1024 devices in a mesh: node: 128 (over z, x), local: 8 (over y, core).
Axes of the slice: x: 4, y: 4, z: 32, core: 2. Of those that a mesh axis runs over, the one named last changes fastest.
Arguments:
- tokens: bfloat16 [1024, 7168], P('node', 'local'), may hold values from -6 to 6
- cotangent: bfloat16 [1024, 7168], P('node', 'local'), may hold values from -6 to 6
- routes: int32 [1024, 2], P('node'), may hold values from 0 to 15, all different within a row; in each aligned block of 8 rows (0 to 7, 8 to 15, ...) at most 2 rows name the same one
- gates: float32 [1024, 2], P('node'), may hold values from 0.2 to 1
- w_gate: bfloat16 [7168, 32768], P('local', 'node'), may hold values from -0.0625 to 0.0625
- w_up: bfloat16 [7168, 32768], P('local', 'node'), may hold values from -0.0625 to 0.0625
- w_down: bfloat16 [32768, 7168], P('node', 'local'), may hold values from -0.125 to 0.125
Outputs:
- mixed: bfloat16 [1024, 7168], P('node', 'local')
- d_tokens: bfloat16 [1024, 7168], P('node', 'local')
- d_gate: bfloat16 [7168, 32768], P('local', 'node')
- d_up: bfloat16 [7168, 32768], P('local', 'node')
- d_down: bfloat16 [32768, 7168], P('node', 'local')
The draws below stay inside these ranges and needn't reach their ends.
Inputs may be any that keep to these rules, and one draw needn't show every extreme that they name: `routes`: each row names 2 different experts; the pairs of one block of 8 rows name one expert at most 2 times, a bound that some block reaches.
All inputs are finite; a program needn't handle non-finite values.
Results may differ from the reference program's by a relative error of at most 0.02.
Values may be sent and summed in bfloat16 or wider, within the bound.
A program may use at most 32 MiB of HBM per device.

```python
import math
import jax
import jax.numpy as jnp
import numpy as np
from jax import lax

D = 7168
FF = 2048
TOP = 2
TOK_NODE = 8
SHARDS = 8
EXP = 16
CAPN = 2
TOKENS = 1024
H_NODE = 256
N_NODE = 128


def block_levels(rng, extent, pieces, least, high):
    level = 1.0
    for axis_at, blocks in pieces:
        heights = jax.random.uniform(jax.random.fold_in(jax.random.fold_in(rng, 6), axis_at), (blocks,), jnp.float32, least / len(pieces), high / len(pieces))
        level = level * jnp.repeat(jnp.exp(heights), extent[axis_at] // blocks).reshape((-1,) + (1,) * (len(extent) - 1 - axis_at))
    return level


def routed_block(rng, own, number, rows, number_of, top, reach, skew):
    ranking = jax.random.permutation(rng, number_of)
    packed, ordinary = shares(number_of, rows * top, reach, skew, True), shares(number_of, rows * top, reach, skew, False)
    places = jnp.arange(number_of)

    def named(lengths, rotation):
        used = int((lengths > 0).sum())
        fixed = max(1, used // 4)
        moved = fixed + (places - fixed + rotation * (used - fixed)) % max(1, number_of - fixed)
        return jnp.zeros((number_of,), jnp.int32).at[ranking[jnp.where(places < fixed, places, moved)]].set(jnp.asarray(lengths, jnp.int32))

    lengths = jnp.where(number % 4 == 0, named(packed, number // 4), named(ordinary, number - number // 4 - 1))
    mixed = jax.random.permutation(jax.random.fold_in(own, 3), number_of)
    donor, sink = mixed[0:number_of // 2 * 2:2], mixed[1:number_of // 2 * 2:2]
    room = jnp.minimum(lengths[donor] - 1, reach - lengths[sink]) // 2
    room = jnp.where((donor == ranking[0]) | (sink == ranking[0]) | (lengths[sink] == 0), 0, jnp.maximum(room, 0))
    moved = jax.random.randint(jax.random.fold_in(own, 4), (number_of // 2,), 0, 1 << 20) % (room + 1)
    lengths = lengths.at[donor].add(-moved).at[sink].add(moved)
    members = jnp.searchsorted(jnp.cumsum(lengths), jnp.arange(rows * top), side="right").astype(jnp.int32)
    table = members.reshape(top, rows).T
    table = table[jax.random.permutation(jax.random.fold_in(own, 1), rows)]
    rotation = jax.random.randint(jax.random.fold_in(own, 2), (rows, 1), 0, top)
    return jnp.take_along_axis(table, (jnp.arange(top)[None, :] + rotation) % top, axis=1)


def shares(count, total, most, slope, full):
    weights = [(1 << 20) // math.isqrt(rank ** slope) + 1 for rank in range(1, count + 1)]
    largest = most if full else min(most, max(-(-total // count), total * weights[0] // sum(weights)))
    least = 1 if total - largest >= count - 1 else 0
    holding, surplus = [largest] + [least] * (count - 1), total - largest - least * (count - 1)
    while surplus > 0:
        free = [i for i in range(1, count) if holding[i] < largest] or [i for i in range(1, count) if holding[i] < most]
        pool, budget = sum([weights[i] for i in free]), surplus
        for i in free:
            extra = min(most - holding[i], max(1, budget * weights[i] // pool), surplus)
            holding[i] = holding[i] + extra
            surplus = surplus - extra
    return np.array(holding)


def scatter_about(key, dims, width, most, shards=(), held_as=jnp.bfloat16):
    entries = width * jax.random.normal(key, dims, jnp.float32)
    if shards:
        entries = entries * block_levels(key, dims, shards, -0.22, 0.18)
    return jnp.clip(entries, -most, most).astype(held_as)


def setup_inputs(seed: int = 0) -> dict:
    key_of = jax.random.split(jax.random.key(seed), 8)
    tokens = scatter_about(key_of[0], (TOKENS, D), 1.0, 6.0, ((0, 128), (1, 8)))
    cotangent = scatter_about(key_of[1], (TOKENS, D), 1.0, 6.0, ((0, 128), (1, 8)))
    routes_keys = jax.random.split(jax.random.fold_in(key_of[2], 1), TOKENS // TOK_NODE)
    routes_turns = jax.random.permutation(jax.random.fold_in(key_of[2], 3), TOKENS // TOK_NODE)
    routes = jax.vmap(lambda own, number: routed_block(jax.random.fold_in(key_of[2], 2), own, number, TOK_NODE, EXP, TOP, CAPN, 2))(routes_keys, routes_turns).reshape((TOKENS, TOP))
    gates = jnp.clip(0.2 + 0.8 * jax.random.uniform(key_of[3], (TOKENS, TOP), jnp.float32) ** block_levels(key_of[3], (TOKENS, TOP), ((0, 128),), -0.2, 0.2), 0.2, 1.0)
    w_gate = scatter_about(key_of[4], (D, EXP * FF), D ** -0.5, 0.0625, ((0, 8), (1, 128)))
    w_up = scatter_about(key_of[5], (D, EXP * FF), D ** -0.5, 0.0625, ((0, 8), (1, 128)))
    w_down = scatter_about(key_of[6], (EXP * FF, D), FF ** -0.5, 0.125, ((0, 128), (1, 8)))
    return {"tokens": tokens, "cotangent": cotangent, "routes": routes, "gates": gates, "w_gate": w_gate, "w_up": w_up, "w_down": w_down}


def slot_tables(routes, gates):
    flat = routes.reshape(N_NODE, TOK_NODE * TOP)
    experts = jnp.arange(EXP, dtype=jnp.int32)
    hot = (flat[:, :, None] == experts[None, None, :]).astype(jnp.int32)
    before = jnp.cumsum(hot, axis=1) - hot
    slot = jnp.sum(before * hot, axis=2)
    slots = jnp.arange(CAPN, dtype=jnp.int32)
    picks = ((flat[:, None, None, :] == experts[None, :, None, None]) & (slot[:, None, None, :] == slots[None, None, :, None])).astype(jnp.float32)
    picks = picks.reshape(N_NODE, EXP, CAPN, TOK_NODE, TOP)
    member = jnp.sum(picks, axis=4)
    weighted = jnp.sum(picks * gates.reshape(N_NODE, 1, 1, TOK_NODE, TOP), axis=4)
    return member, weighted


def expert_pass(index, slot_tokens, slot_grads, w_gate, w_up, w_down):
    rows_x = slot_tokens[index]
    rows_g = slot_grads[index]
    wg = lax.dynamic_slice_in_dim(w_gate, index * FF, FF, 1)
    wu = lax.dynamic_slice_in_dim(w_up, index * FF, FF, 1)
    wd = lax.dynamic_slice_in_dim(w_down, index * FF, FF, 0)
    a_val = jnp.dot(rows_x, wg, preferred_element_type=jnp.float32)
    b_val = jnp.dot(rows_x, wu, preferred_element_type=jnp.float32)
    sig = jax.nn.sigmoid(a_val)
    hidden = (a_val * sig * b_val).astype(jnp.bfloat16)
    dh_val = jnp.dot(rows_g, wd.T, preferred_element_type=jnp.float32)
    grad_down = jnp.dot(hidden.T, rows_g, preferred_element_type=jnp.float32).astype(jnp.bfloat16)
    grad_a = (dh_val * b_val * sig * (1.0 + a_val * (1.0 - sig))).astype(jnp.bfloat16)
    grad_b = (dh_val * a_val * sig).astype(jnp.bfloat16)
    grad_gate = jnp.dot(rows_x.T, grad_a, preferred_element_type=jnp.float32).astype(jnp.bfloat16)
    grad_up = jnp.dot(rows_x.T, grad_b, preferred_element_type=jnp.float32).astype(jnp.bfloat16)

    def group_step(carry, group):
        out_sum, dx_sum = carry
        start = group * H_NODE
        h_part = lax.dynamic_slice_in_dim(hidden, start, H_NODE, 1)
        d_part = lax.dynamic_slice_in_dim(wd, start, H_NODE, 0)
        out_part = jnp.dot(h_part, d_part, preferred_element_type=jnp.float32).astype(jnp.bfloat16)
        ga = lax.dynamic_slice_in_dim(grad_a, start, H_NODE, 1)
        gb = lax.dynamic_slice_in_dim(grad_b, start, H_NODE, 1)
        wg_part = lax.dynamic_slice_in_dim(wg, start, H_NODE, 1)
        wu_part = lax.dynamic_slice_in_dim(wu, start, H_NODE, 1)
        dx_part = (jnp.dot(ga, wg_part.T, preferred_element_type=jnp.float32) + jnp.dot(gb, wu_part.T, preferred_element_type=jnp.float32)).astype(jnp.bfloat16)
        return (out_sum + out_part.astype(jnp.float32), dx_sum + dx_part.astype(jnp.float32)), None

    zeros = jnp.zeros((N_NODE * CAPN, D), jnp.float32)
    (out_sum, dx_sum), _ = lax.scan(group_step, (zeros, zeros), jnp.arange(SHARDS, dtype=jnp.int32))
    return out_sum, dx_sum, grad_gate, grad_up, grad_down


def reference(tokens, cotangent, routes, gates, w_gate, w_up, w_down):
    member, weighted = slot_tables(routes, gates)
    blocks_x = tokens.reshape(N_NODE, TOK_NODE, D).astype(jnp.float32)
    blocks_g = cotangent.reshape(N_NODE, TOK_NODE, D).astype(jnp.float32)
    slot_tokens = jnp.einsum("necs,nsd->encd", member, blocks_x).astype(jnp.bfloat16).reshape(EXP, N_NODE * CAPN, D)
    slot_grads = jnp.einsum("necs,nsd->encd", weighted, blocks_g).astype(jnp.bfloat16).reshape(EXP, N_NODE * CAPN, D)
    outs, dxs, grad_gate, grad_up, grad_down = lax.map(lambda index: expert_pass(index, slot_tokens, slot_grads, w_gate, w_up, w_down), jnp.arange(EXP, dtype=jnp.int32))
    outs = outs.reshape(EXP, N_NODE, CAPN, D)
    dxs = dxs.reshape(EXP, N_NODE, CAPN, D)
    mixed = jnp.einsum("necs,encd->nsd", weighted, outs).reshape(TOKENS, D).astype(jnp.bfloat16)
    d_tokens = jnp.einsum("necs,encd->nsd", member, dxs).reshape(TOKENS, D).astype(jnp.bfloat16)
    d_gate = jnp.transpose(grad_gate, (1, 0, 2)).reshape(D, EXP * FF)
    d_up = jnp.transpose(grad_up, (1, 0, 2)).reshape(D, EXP * FF)
    d_down = grad_down.reshape(EXP * FF, D)
    return mixed, d_tokens, d_gate, d_up, d_down
```

```python
import functools

import jax
import jax.numpy as jnp
from jax import lax
from jax.experimental import pallas as pl
from jax.experimental.pallas import tpu as pltpu
from jax.sharding import PartitionSpec as P

MESH = pl.DeviceIdType.MESH
BF = jnp.bfloat16
F32 = jnp.float32
I32 = jnp.int32
EXPERTS = 16
UNIT = 16

(DX, DG, GX, GG, SAB, SDH, AH, AD, RO, RX, BO, BX) = range(12)


def iotas(shape):
    return lax.broadcasted_iota(I32, shape, 0), lax.broadcasted_iota(I32, shape, 1)


def pick_table(rows, cols, routes, gates):
    expert, token = rows >> 4, cols & 7
    hot = jnp.zeros(rows.shape, F32)
    before = jnp.zeros(rows.shape, F32)
    gate = jnp.zeros(rows.shape, F32)
    for t in range(8):
        first, second = expert == routes[0, t], expert == routes[1, t]
        here = token == t
        named = jnp.where(first | second, 1.0, 0.0)
        hot = hot + jnp.where(here, named, 0.0)
        before = before + jnp.where(token > t, named, 0.0)
        weight = jnp.where(first, gates[0, t], 0.0) + jnp.where(second, gates[1, t], 0.0)
        gate = gate + jnp.where(here, weight, 0.0)
    slot = (rows & 1).astype(F32)
    keep = (((rows & 15) >> 1) == (cols >> 3)) & (before == slot)
    return jnp.where(keep, hot, 0.0), jnp.where(keep, gate, 0.0)


def stacked(value, chunks):
    parts = [value[:, j * 128 : (j + 1) * 128] for j in range(chunks)]
    parts = parts + [jnp.zeros_like(parts[0])] * (8 - chunks)
    return jnp.concatenate(parts, axis=0)


def kernel(
    sizes,
    tokens, cot, routes, gates, w_gate, w_up, w_down,
    mixed, d_tokens, d_gate, d_up, d_down,
    slot_x, slot_g, got_x, got_g, all_x, all_g, w_in, w_out,
    part_ab, sum_ab, part_dh, sum_dh, hid, grads,
    out_s, out_r, dx_s, dx_r, back_os, back_or, back_xs, back_xr,
    grad_in, grad_out, spread,
    send, recv, loads,
):
    ne, ns, nl = sizes
    width = tokens.shape[1]
    chunks = width // 128
    hidden_n = w_gate.shape[1]
    per = ne * 2
    rows_all = per * ns
    piece = rows_all // nl
    node, loc = lax.axis_index("node"), lax.axis_index("local")
    expert, shard = node // ns, node % ns

    fetch = [
        pltpu.make_async_copy(w_gate, w_in.at[:, pl.ds(0, hidden_n)], loads.at[0]),
        pltpu.make_async_copy(w_up, w_in.at[:, pl.ds(hidden_n, hidden_n)], loads.at[1]),
        pltpu.make_async_copy(w_down, w_out, loads.at[2]),
    ]
    for copy in fetch:
        copy.start()

    far = sorted(range(1, ne), key=lambda d: -min(d, ne - d))
    by_expert = [(lax.rem(expert + d, ne) * ns + shard, loc, lax.rem(expert + d, ne)) for d in far]
    by_shard = []
    for d in range(1, ns):
        other = lax.rem(shard + d, ns)
        by_shard.append((expert * ns + other, loc, other))
    by_local = []
    for d in range(1, nl):
        other = lax.rem(loc + d, nl)
        by_local.append((node, other, other))

    barrier = pltpu.get_barrier_semaphore()
    everyone = by_expert + by_shard + by_local
    for to_node, to_loc, _ in everyone:
        pl.semaphore_signal(
            barrier, inc=1, device_id={"node": to_node, "local": to_loc}, device_id_type=MESH
        )

    def push(phase, peers, source, target):
        for to_node, to_loc, index in peers:
            pltpu.make_async_remote_copy(
                src_ref=source(index),
                dst_ref=target(index),
                send_sem=send.at[phase],
                recv_sem=recv.at[phase],
                device_id={"node": to_node, "local": to_loc},
                device_id_type=MESH,
            ).start()

    def arrived(phase, ref, count):
        if count:
            part = ref.at[pl.ds(0, count)]
            pltpu.make_async_copy(part, part, recv.at[phase]).wait()

    def sent(phase, ref, count):
        if count:
            part = ref.at[pl.ds(0, count)]
            pltpu.make_async_copy(part, part, send.at[phase]).wait()

    def rows(ref, index, n):
        return ref.at[pl.ds(pl.multiple_of(index * n, n), n)]

    unit_rows = ne * UNIT
    member, weighted = pick_table(*iotas((unit_rows, 64)), routes, gates)
    pick = member.astype(BF)
    slot_gate = jnp.sum(weighted, axis=1, keepdims=True)
    tok = stacked(tokens[...].astype(F32), chunks).astype(BF)
    slot_x[...] = jnp.dot(pick, tok, preferred_element_type=F32).astype(BF)
    grad_rows = stacked(cot[...].astype(F32), chunks).astype(BF)
    slot_g[...] = (jnp.dot(pick, grad_rows, preferred_element_type=F32) * slot_gate).astype(BF)

    pl.semaphore_wait(barrier, len(everyone))
    push(DX, by_expert, lambda e: rows(slot_x, e, UNIT), lambda e: rows(got_x, expert, UNIT))
    push(DG, by_expert, lambda e: rows(slot_g, e, UNIT), lambda e: rows(got_g, expert, UNIT))
    own_unit = pl.ds(pl.multiple_of(expert * UNIT, UNIT), UNIT)
    got_x[own_unit, :] = slot_x[own_unit, :]
    got_g[own_unit, :] = slot_g[own_unit, :]

    a, b = iotas((chunks * per, unit_rows))
    q = lax.rem(a, per)
    spread[...] = jnp.where(b == (q >> 1) * UNIT + 2 * (a // per) + (q & 1), 1.0, 0.0).astype(BF)

    own_rows = pl.ds(pl.multiple_of(shard * per, per), per)

    def unfold(ref, target):
        flat = jnp.dot(spread[...], ref[...], preferred_element_type=F32).astype(BF)
        for j in range(chunks):
            target[own_rows, j * 128 : (j + 1) * 128] = flat[j * per : (j + 1) * per, :]

    arrived(DX, got_x, (ne - 1) * UNIT)
    unfold(got_x, all_x)
    push(GX, by_shard, lambda s: all_x.at[own_rows], lambda s: all_x.at[own_rows])
    arrived(DG, got_g, (ne - 1) * UNIT)
    unfold(got_g, all_g)
    push(GG, by_shard, lambda s: all_g.at[own_rows], lambda s: all_g.at[own_rows])

    for copy in fetch:
        copy.wait()
    arrived(GX, all_x, (ns - 1) * per)
    part_ab[...] = jnp.dot(all_x[...], w_in[...], preferred_element_type=F32).astype(BF)
    push(SAB, by_local, lambda l: rows(part_ab, l, piece), lambda l: rows(sum_ab, loc, piece))
    mine = pl.ds(pl.multiple_of(loc * piece, piece), piece)
    sum_ab[mine, :] = part_ab[mine, :]

    arrived(GG, all_g, (ns - 1) * per)
    part_dh[...] = lax.dot_general(
        all_g[...], w_out[...], (((1,), (1,)), ((), ())), preferred_element_type=F32
    ).astype(BF)
    push(SDH, by_local, lambda l: rows(part_dh, l, piece), lambda l: rows(sum_dh, loc, piece))
    sum_dh[mine, :] = part_dh[mine, :]

    def total(ref, n, count):
        value = ref[0:n, :].astype(F32)
        for i in range(1, count):
            value = value + ref[i * n : (i + 1) * n, :].astype(F32)
        return value

    arrived(SAB, sum_ab, (nl - 1) * piece)
    ab = total(sum_ab, piece, nl)
    a_val, b_val = ab[:, :hidden_n], ab[:, hidden_n:]
    sig = jax.nn.sigmoid(a_val)
    hid[mine, :] = (a_val * sig * b_val).astype(BF)
    push(AH, by_local, lambda l: hid.at[mine], lambda l: hid.at[mine])

    arrived(SDH, sum_dh, (nl - 1) * piece)
    dh = total(sum_dh, piece, nl)
    grads[mine, 0:hidden_n] = (dh * b_val * sig * (1.0 + a_val * (1.0 - sig))).astype(BF)
    grads[mine, hidden_n : 2 * hidden_n] = (dh * a_val * sig).astype(BF)
    push(AD, by_local, lambda l: grads.at[mine], lambda l: grads.at[mine])

    arrived(AH, hid, (nl - 1) * piece)
    out_s[...] = jnp.dot(hid[...], w_out[...], preferred_element_type=F32).astype(BF)
    push(RO, by_shard, lambda s: rows(out_s, s, per), lambda s: rows(out_r, shard, per))
    out_r[own_rows, :] = out_s[own_rows, :]

    arrived(AD, grads, (nl - 1) * piece)
    dx_s[...] = lax.dot_general(
        grads[...], w_in[...], (((1,), (1,)), ((), ())), preferred_element_type=F32
    ).astype(BF)
    push(RX, by_shard, lambda s: rows(dx_s, s, per), lambda s: rows(dx_r, shard, per))
    dx_r[own_rows, :] = dx_s[own_rows, :]

    def fold(ref):
        value = total(ref, per, ns).astype(BF)
        tall = jnp.concatenate([value[:, j * 128 : (j + 1) * 128] for j in range(chunks)], axis=0)
        return lax.dot_general(
            spread[...], tall, (((0,), (0,)), ((), ())), preferred_element_type=F32
        ).astype(BF)

    arrived(RO, out_r, (ns - 1) * per)
    back_os[...] = fold(out_r)
    push(BO, by_expert, lambda e: rows(back_os, e, UNIT), lambda e: rows(back_or, expert, UNIT))
    back_or[own_unit, :] = back_os[own_unit, :]

    over_rows = (((0,), (0,)), ((), ()))
    grad_out[...] = lax.dot_general(
        hid[...], all_g[...], over_rows, preferred_element_type=F32
    ).astype(BF)
    grad_in[...] = lax.dot_general(
        all_x[...], grads[...], over_rows, preferred_element_type=F32
    ).astype(BF)
    store = [
        pltpu.make_async_copy(grad_in.at[:, pl.ds(0, hidden_n)], d_gate, loads.at[3]),
        pltpu.make_async_copy(grad_in.at[:, pl.ds(hidden_n, hidden_n)], d_up, loads.at[4]),
        pltpu.make_async_copy(grad_out, d_down, loads.at[5]),
    ]
    for copy in store:
        copy.start()

    arrived(RX, dx_r, (ns - 1) * per)
    back_xs[...] = fold(dx_r)
    push(BX, by_expert, lambda e: rows(back_xs, e, UNIT), lambda e: rows(back_xr, expert, UNIT))
    back_xr[own_unit, :] = back_xs[own_unit, :]

    cols, tall_rows = iotas((64, unit_rows))
    member_t, weighted_t = pick_table(tall_rows, cols, routes, gates)
    high = weighted_t.astype(BF)
    low = (weighted_t - high.astype(F32)).astype(BF)

    arrived(BO, back_or, (ne - 1) * UNIT)
    value = back_or[...]
    flat = jnp.dot(high, value, preferred_element_type=F32) + jnp.dot(
        low, value, preferred_element_type=F32
    )
    for j in range(chunks):
        mixed[:, j * 128 : (j + 1) * 128] = flat[j * 8 : (j + 1) * 8, :].astype(BF)
    arrived(BX, back_xr, (ne - 1) * UNIT)
    flat = jnp.dot(member_t.astype(BF), back_xr[...], preferred_element_type=F32)
    for j in range(chunks):
        d_tokens[:, j * 128 : (j + 1) * 128] = flat[j * 8 : (j + 1) * 8, :].astype(BF)

    sent(DX, slot_x, (ne - 1) * UNIT)
    sent(DG, slot_g, (ne - 1) * UNIT)
    sent(GX, all_x, (ns - 1) * per)
    sent(GG, all_g, (ns - 1) * per)
    sent(SAB, part_ab, (nl - 1) * piece)
    sent(SDH, part_dh, (nl - 1) * piece)
    sent(AH, hid, (nl - 1) * piece)
    sent(AD, grads, (nl - 1) * piece)
    sent(RO, out_s, (ns - 1) * per)
    sent(RX, dx_s, (ns - 1) * per)
    sent(BO, back_os, (ne - 1) * UNIT)
    sent(BX, back_xs, (ne - 1) * UNIT)
    for copy in store:
        copy.wait()


def local(sizes, tokens, cotangent, routes, gates, w_gate, w_up, w_down):
    ne, ns, nl = sizes
    toks, width = tokens.shape
    hidden_n = w_gate.shape[1]
    per = ne * 2
    rows_all = per * ns
    chunks = width // 128
    unit_rows = ne * UNIT
    vmem = pl.BlockSpec(memory_space=pltpu.VMEM)
    smem = pl.BlockSpec(memory_space=pltpu.SMEM)
    anywhere = pl.BlockSpec(memory_space=pl.ANY)
    unit = pltpu.VMEM((unit_rows, 128), BF)
    wide = pltpu.VMEM((rows_all, width), BF)
    scratch = (
        [unit] * 4
        + [wide] * 2
        + [pltpu.VMEM((width, 2 * hidden_n), BF), pltpu.VMEM((hidden_n, width), BF)]
        + [pltpu.VMEM((rows_all, 2 * hidden_n), BF)] * 2
        + [pltpu.VMEM((rows_all, hidden_n), BF)] * 2
        + [pltpu.VMEM((rows_all, hidden_n), BF), pltpu.VMEM((rows_all, 2 * hidden_n), BF)]
        + [wide] * 4
        + [unit] * 4
        + [pltpu.VMEM((width, 2 * hidden_n), BF), pltpu.VMEM((hidden_n, width), BF)]
        + [pltpu.VMEM((chunks * per, unit_rows), BF)]
        + [pltpu.SemaphoreType.DMA((12,)), pltpu.SemaphoreType.DMA((12,)), pltpu.SemaphoreType.DMA((6,))]
    )
    return pl.pallas_call(
        functools.partial(kernel, sizes),
        out_shape=(
            jax.ShapeDtypeStruct(tokens.shape, BF),
            jax.ShapeDtypeStruct(tokens.shape, BF),
            jax.ShapeDtypeStruct(w_gate.shape, BF),
            jax.ShapeDtypeStruct(w_up.shape, BF),
            jax.ShapeDtypeStruct(w_down.shape, BF),
        ),
        in_specs=[vmem, vmem, smem, smem, anywhere, anywhere, anywhere],
        out_specs=(vmem, vmem, anywhere, anywhere, anywhere),
        scratch_shapes=scratch,
        compiler_params=pltpu.CompilerParams(
            collective_id=0, has_side_effects=True, vmem_limit_bytes=32 * 1024 * 1024
        ),
        cost_estimate=pl.CostEstimate(flops=1_100_000_000, bytes_accessed=3_000_000, transcendentals=8192),
    )(tokens, cotangent, routes.T, gates.T, w_gate, w_up, w_down)


def build(mesh, experts):
    shards = mesh.shape["node"] // experts
    sizes = (experts, shards, mesh.shape["local"])
    return jax.shard_map(
        functools.partial(local, sizes),
        mesh=mesh,
        in_specs=(
            P("node", "local"),
            P("node", "local"),
            P("node", None),
            P("node", None),
            P("local", "node"),
            P("local", "node"),
            P("node", "local"),
        ),
        out_specs=(
            P("node", "local"),
            P("node", "local"),
            P("local", "node"),
            P("local", "node"),
            P("node", "local"),
        ),
        check_vma=False,
    )


def solution(mesh):
    return build(mesh, EXPERTS)
```

```python
import functools

import jax
import jax.numpy as jnp
from jax import lax
from jax.experimental import pallas as pl
from jax.experimental.pallas import tpu as pltpu
from jax.sharding import PartitionSpec as P

MESH = pl.DeviceIdType.MESH
BF = jnp.bfloat16
F32 = jnp.float32
I32 = jnp.int32
EXPERTS = 16
UNIT = 16

(DX, DG, GX, GG, SAB, SDH, AH, AD, RO, RX, BO, BX, UX, LX, UG, LG) = range(16)


def iotas(shape):
    return lax.broadcasted_iota(I32, shape, 0), lax.broadcasted_iota(I32, shape, 1)


def pick_table(rows, cols, mine, ne, routes, gates):
    expert, token = (rows >> 4) + mine, cols & 7
    expert = jnp.where(expert >= ne, expert - ne, expert)
    hot = jnp.zeros(rows.shape, F32)
    before = jnp.zeros(rows.shape, F32)
    gate = jnp.zeros(rows.shape, F32)
    for t in range(8):
        first, second = expert == routes[0, t], expert == routes[1, t]
        here = token == t
        named = jnp.where(first | second, 1.0, 0.0)
        hot = hot + jnp.where(here, named, 0.0)
        before = before + jnp.where(token > t, named, 0.0)
        weight = jnp.where(first, gates[0, t], 0.0) + jnp.where(second, gates[1, t], 0.0)
        gate = gate + jnp.where(here, weight, 0.0)
    slot = (rows & 1).astype(F32)
    keep = (((rows & 15) >> 1) == (cols >> 3)) & (before == slot)
    return jnp.where(keep, hot, 0.0), jnp.where(keep, gate, 0.0)


def stacked(value, chunks):
    parts = [value[:, j * 128 : (j + 1) * 128] for j in range(chunks)]
    parts = parts + [jnp.zeros_like(parts[0])] * (8 - chunks)
    return jnp.concatenate(parts, axis=0)


def kernel(
    sizes,
    tokens_in, cot_in, routes_in, gates_in, w_gate, w_up, w_down,
    mixed, d_tokens, d_gate, d_up, d_down,
    tokens, cot, routes, gates,
    slot_x, slot_g, got_x, got_g, via_x, via_g, all_x, all_g, w_in, w_out,
    part_ab, sum_ab, part_dh, sum_dh, hid, grads,
    out_s, out_r, dx_s, dx_r, back_os, back_or, back_xs, back_xr,
    grad_in, grad_out, spread,
    send, recv, loads,
):
    ne, ns, nl = sizes
    width = tokens.shape[1]
    chunks = width // 128
    hidden_n = w_gate.shape[1]
    per = ne * 2
    rows_all = per * ns
    piece = rows_all // nl
    node, loc = lax.axis_index("node"), lax.axis_index("local")
    expert, shard = node // ns, node % ns

    first = [
        pltpu.make_async_copy(routes_in, routes, loads.at[6]),
        pltpu.make_async_copy(gates_in, gates, loads.at[7]),
        pltpu.make_async_copy(tokens_in, tokens, loads.at[8]),
        pltpu.make_async_copy(cot_in, cot, loads.at[9]),
    ]
    fetch = [
        pltpu.make_async_copy(w_gate, w_in.at[:, pl.ds(0, hidden_n)], loads.at[0]),
        pltpu.make_async_copy(w_up, w_in.at[:, pl.ds(hidden_n, hidden_n)], loads.at[1]),
        pltpu.make_async_copy(w_down, w_out, loads.at[2]),
    ]
    for copy in first + fetch:
        copy.start()

    leg = ne // 4
    up, low = ne // 2, (ne - 1) // 2
    near = list(range(1, leg + 1)) + list(range(ne - leg, ne))

    def at_expert(d):
        return lax.rem(expert + d, ne) * ns + shard, loc

    far = sorted(range(1, ne), key=lambda d: -min(d, ne - d))
    by_shard = []
    for d in range(1, ns):
        other = lax.rem(shard + d, ns)
        by_shard.append((expert * ns + other, loc, other))
    by_local = []
    for d in range(1, nl):
        other = lax.rem(loc + d, nl)
        by_local.append((node, other, other))

    barrier = pltpu.get_barrier_semaphore()
    everyone = [(*at_expert(d), d) for d in near] + by_shard + by_local
    for to_node, to_loc, _ in everyone:
        pl.semaphore_signal(
            barrier, inc=1, device_id={"node": to_node, "local": to_loc}, device_id_type=MESH
        )

    def push(phase, peers, source, target):
        for to_node, to_loc, index in peers:
            pltpu.make_async_remote_copy(
                src_ref=source(index),
                dst_ref=target(index),
                send_sem=send.at[phase],
                recv_sem=recv.at[phase],
                device_id={"node": to_node, "local": to_loc},
                device_id_type=MESH,
            ).start()

    def arrived(phase, ref, count):
        if count:
            part = ref.at[pl.ds(0, count)]
            pltpu.make_async_copy(part, part, recv.at[phase]).wait()

    def sent(phase, ref, count):
        if count:
            part = ref.at[pl.ds(0, count)]
            pltpu.make_async_copy(part, part, send.at[phase]).wait()

    def rows(ref, index, n):
        return ref.at[pl.ds(pl.multiple_of(index * n, n), n)]

    def units(ref, index, count=1):
        return ref.at[pl.ds(index * UNIT, count * UNIT)]

    def ship(phase, d, source, target):
        push(phase, [(*at_expert(d), 0)], lambda _: source, lambda _: target)

    for copy in first:
        copy.wait()
    unit_rows = ne * UNIT
    member, weighted = pick_table(*iotas((unit_rows, 64)), expert, ne, routes, gates)
    pick = member.astype(BF)
    slot_gate = jnp.sum(weighted, axis=1, keepdims=True)
    tok = stacked(tokens[...].astype(F32), chunks).astype(BF)
    slot_x[...] = jnp.dot(pick, tok, preferred_element_type=F32).astype(BF)
    grad_rows = stacked(cot[...].astype(F32), chunks).astype(BF)
    slot_g[...] = (jnp.dot(pick, grad_rows, preferred_element_type=F32) * slot_gate).astype(BF)

    pl.semaphore_wait(barrier, len(everyone))
    n_up, n_low = up - leg, low - leg
    for slots, got, via, straight, above, below in (
        (slot_x, got_x, via_x, DX, UX, LX),
        (slot_g, got_g, via_g, DG, UG, LG),
    ):
        ship(above, leg, units(slots, leg + 1, n_up), units(via, 0, n_up))
        if n_low:
            ship(below, ne - leg, units(slots, up + 1, n_low), units(via, n_up, n_low))
        for d in sorted(near, key=lambda d: -min(d, ne - d)):
            ship(straight, d, units(slots, d), units(got, d))
        got[0:UNIT, :] = slots[0:UNIT, :]

    a, b = iotas((chunks * per, unit_rows))
    q = lax.rem(a, per)
    spread[...] = jnp.where(b == (q >> 1) * UNIT + 2 * (a // per) + (q & 1), 1.0, 0.0).astype(BF)

    own_rows = pl.ds(pl.multiple_of(shard * per, per), per)

    def unfold(ref, target):
        flat = jnp.dot(spread[...], ref[...], preferred_element_type=F32).astype(BF)
        for j in range(chunks):
            target[own_rows, j * 128 : (j + 1) * 128] = flat[j * per : (j + 1) * per, :]

    for got, via, straight, above, below in ((got_x, via_x, DX, UX, LX), (got_g, via_g, DG, UG, LG)):
        arrived(above, via, n_up * UNIT)
        for i in reversed(range(n_up)):
            ship(straight, i + 1, units(via, i), units(got, leg + 1 + i))
        arrived(below, via, n_low * UNIT)
        for i in range(n_low):
            ship(straight, ne - (n_low - i), units(via, n_up + i), units(got, up + 1 + i))

    arrived(DX, got_x, (ne - 1) * UNIT)
    unfold(got_x, all_x)
    push(GX, by_shard, lambda s: all_x.at[own_rows], lambda s: all_x.at[own_rows])
    arrived(DG, got_g, (ne - 1) * UNIT)
    unfold(got_g, all_g)
    push(GG, by_shard, lambda s: all_g.at[own_rows], lambda s: all_g.at[own_rows])

    for copy in fetch:
        copy.wait()
    arrived(GX, all_x, (ns - 1) * per)
    part_ab[...] = jnp.dot(all_x[...], w_in[...], preferred_element_type=F32).astype(BF)
    push(SAB, by_local, lambda l: rows(part_ab, l, piece), lambda l: rows(sum_ab, loc, piece))
    mine = pl.ds(pl.multiple_of(loc * piece, piece), piece)
    sum_ab[mine, :] = part_ab[mine, :]

    arrived(GG, all_g, (ns - 1) * per)
    part_dh[...] = lax.dot_general(
        all_g[...], w_out[...], (((1,), (1,)), ((), ())), preferred_element_type=F32
    ).astype(BF)
    push(SDH, by_local, lambda l: rows(part_dh, l, piece), lambda l: rows(sum_dh, loc, piece))
    sum_dh[mine, :] = part_dh[mine, :]

    def total(ref, n, count):
        value = ref[0:n, :].astype(F32)
        for i in range(1, count):
            value = value + ref[i * n : (i + 1) * n, :].astype(F32)
        return value

    arrived(SAB, sum_ab, (nl - 1) * piece)
    ab = total(sum_ab, piece, nl)
    a_val, b_val = ab[:, :hidden_n], ab[:, hidden_n:]
    sig = jax.nn.sigmoid(a_val)
    hid[mine, :] = (a_val * sig * b_val).astype(BF)
    push(AH, by_local, lambda l: hid.at[mine], lambda l: hid.at[mine])

    arrived(SDH, sum_dh, (nl - 1) * piece)
    dh = total(sum_dh, piece, nl)
    grads[mine, 0:hidden_n] = (dh * b_val * sig * (1.0 + a_val * (1.0 - sig))).astype(BF)
    grads[mine, hidden_n : 2 * hidden_n] = (dh * a_val * sig).astype(BF)
    push(AD, by_local, lambda l: grads.at[mine], lambda l: grads.at[mine])

    arrived(AH, hid, (nl - 1) * piece)
    out_s[...] = jnp.dot(hid[...], w_out[...], preferred_element_type=F32).astype(BF)
    push(RO, by_shard, lambda s: rows(out_s, s, per), lambda s: rows(out_r, shard, per))
    out_r[own_rows, :] = out_s[own_rows, :]

    arrived(AD, grads, (nl - 1) * piece)
    dx_s[...] = lax.dot_general(
        grads[...], w_in[...], (((1,), (1,)), ((), ())), preferred_element_type=F32
    ).astype(BF)
    push(RX, by_shard, lambda s: rows(dx_s, s, per), lambda s: rows(dx_r, shard, per))
    dx_r[own_rows, :] = dx_s[own_rows, :]

    def fold(ref):
        value = total(ref, per, ns).astype(BF)
        tall = jnp.concatenate([value[:, j * 128 : (j + 1) * 128] for j in range(chunks)], axis=0)
        return lax.dot_general(
            spread[...], tall, (((0,), (0,)), ((), ())), preferred_element_type=F32
        ).astype(BF)

    arrived(RO, out_r, (ns - 1) * per)
    back_os[...] = fold(out_r)
    for d in far:
        ship(BO, ne - d, units(back_os, d), units(back_or, d))
    back_or[0:UNIT, :] = back_os[0:UNIT, :]

    over_rows = (((0,), (0,)), ((), ()))
    grad_out[...] = lax.dot_general(
        hid[...], all_g[...], over_rows, preferred_element_type=F32
    ).astype(BF)
    grad_in[...] = lax.dot_general(
        all_x[...], grads[...], over_rows, preferred_element_type=F32
    ).astype(BF)
    store = [
        pltpu.make_async_copy(grad_in.at[:, pl.ds(0, hidden_n)], d_gate, loads.at[3]),
        pltpu.make_async_copy(grad_in.at[:, pl.ds(hidden_n, hidden_n)], d_up, loads.at[4]),
        pltpu.make_async_copy(grad_out, d_down, loads.at[5]),
    ]
    for copy in store:
        copy.start()

    arrived(RX, dx_r, (ns - 1) * per)
    back_xs[...] = fold(dx_r)
    for d in far:
        ship(BX, ne - d, units(back_xs, d), units(back_xr, d))
    back_xr[0:UNIT, :] = back_xs[0:UNIT, :]

    cols, tall_rows = iotas((64, unit_rows))
    member_t, weighted_t = pick_table(tall_rows, cols, expert, ne, routes, gates)
    high = weighted_t.astype(BF)
    low = (weighted_t - high.astype(F32)).astype(BF)

    arrived(BO, back_or, (ne - 1) * UNIT)
    value = back_or[...]
    flat = jnp.dot(high, value, preferred_element_type=F32) + jnp.dot(
        low, value, preferred_element_type=F32
    )
    for j in range(chunks):
        mixed[:, j * 128 : (j + 1) * 128] = flat[j * 8 : (j + 1) * 8, :].astype(BF)
    arrived(BX, back_xr, (ne - 1) * UNIT)
    flat = jnp.dot(member_t.astype(BF), back_xr[...], preferred_element_type=F32)
    for j in range(chunks):
        d_tokens[:, j * 128 : (j + 1) * 128] = flat[j * 8 : (j + 1) * 8, :].astype(BF)

    for phase in (DX, DG):
        sent(phase, slot_x, (ne - 1) * UNIT)
    for above, below in ((UX, LX), (UG, LG)):
        sent(above, via_x, n_up * UNIT)
        sent(below, via_x, n_low * UNIT)
    sent(GX, all_x, (ns - 1) * per)
    sent(GG, all_g, (ns - 1) * per)
    sent(SAB, part_ab, (nl - 1) * piece)
    sent(SDH, part_dh, (nl - 1) * piece)
    sent(AH, hid, (nl - 1) * piece)
    sent(AD, grads, (nl - 1) * piece)
    sent(RO, out_s, (ns - 1) * per)
    sent(RX, dx_s, (ns - 1) * per)
    sent(BO, back_os, (ne - 1) * UNIT)
    sent(BX, back_xs, (ne - 1) * UNIT)
    for copy in store:
        copy.wait()


def place(*refs):
    count = len(refs) // 2
    done = refs[-1]
    copies = [pltpu.make_async_copy(refs[i], refs[count + i], done.at[i]) for i in range(count)]
    for copy in copies:
        copy.start()
    for copy in copies:
        copy.wait()


def local(sizes, tokens, cotangent, routes, gates, w_gate, w_up, w_down):
    ne, ns, nl = sizes
    toks, width = tokens.shape
    hidden_n = w_gate.shape[1]
    per = ne * 2
    rows_all = per * ns
    chunks = width // 128
    unit_rows = ne * UNIT
    vmem = pl.BlockSpec(memory_space=pltpu.VMEM)
    anywhere = pl.BlockSpec(memory_space=pl.ANY)
    unit = pltpu.VMEM((unit_rows, 128), BF)
    wide = pltpu.VMEM((rows_all, width), BF)
    scratch = (
        [pltpu.VMEM(tokens.shape, BF)] * 2
        + [pltpu.SMEM((2, toks), I32), pltpu.SMEM((2, toks), F32)]
        + [unit] * 4
        + [pltpu.VMEM((max(2, ne // 2 - 1) * UNIT, 128), BF)] * 2
        + [wide] * 2
        + [pltpu.VMEM((width, 2 * hidden_n), BF), pltpu.VMEM((hidden_n, width), BF)]
        + [pltpu.VMEM((rows_all, 2 * hidden_n), BF)] * 2
        + [pltpu.VMEM((rows_all, hidden_n), BF)] * 2
        + [pltpu.VMEM((rows_all, hidden_n), BF), pltpu.VMEM((rows_all, 2 * hidden_n), BF)]
        + [wide] * 4
        + [unit] * 4
        + [pltpu.VMEM((width, 2 * hidden_n), BF), pltpu.VMEM((hidden_n, width), BF)]
        + [pltpu.VMEM((chunks * per, unit_rows), BF)]
        + [pltpu.SemaphoreType.DMA((16,)), pltpu.SemaphoreType.DMA((16,)), pltpu.SemaphoreType.DMA((10,))]
    )
    shapes = (
            jax.ShapeDtypeStruct(tokens.shape, BF),
            jax.ShapeDtypeStruct(tokens.shape, BF),
            jax.ShapeDtypeStruct(w_gate.shape, BF),
            jax.ShapeDtypeStruct(w_up.shape, BF),
            jax.ShapeDtypeStruct(w_down.shape, BF),
    )
    results = pl.pallas_call(
        functools.partial(kernel, sizes),
        out_shape=shapes,
        in_specs=[anywhere] * 7,
        out_specs=(vmem, vmem, anywhere, anywhere, anywhere),
        scratch_shapes=scratch,
        compiler_params=pltpu.CompilerParams(
            collective_id=0, has_side_effects=True, vmem_limit_bytes=60 * 1024 * 1024
        ),
        cost_estimate=pl.CostEstimate(flops=1_100_000_000, bytes_accessed=3_000_000, transcendentals=8192),
    )(tokens, cotangent, routes.T, gates.T, w_gate, w_up, w_down)
    return pl.pallas_call(
        place,
        out_shape=shapes,
        in_specs=[anywhere] * 5,
        out_specs=(anywhere,) * 5,
        scratch_shapes=[pltpu.SemaphoreType.DMA((5,))],
    )(*results)


def build(mesh, experts):
    shards = mesh.shape["node"] // experts
    sizes = (experts, shards, mesh.shape["local"])
    return jax.shard_map(
        functools.partial(local, sizes),
        mesh=mesh,
        in_specs=(
            P("node", "local"),
            P("node", "local"),
            P("node", None),
            P("node", None),
            P("local", "node"),
            P("local", "node"),
            P("node", "local"),
        ),
        out_specs=(
            P("node", "local"),
            P("node", "local"),
            P("local", "node"),
            P("local", "node"),
            P("node", "local"),
        ),
        check_vma=False,
    )


def solution(mesh):
    return build(mesh, EXPERTS)
```

```python
import functools

import jax
import jax.numpy as jnp
from jax import lax
from jax.experimental import pallas as pl
from jax.experimental.pallas import tpu as pltpu
from jax.sharding import PartitionSpec as P

MESH = pl.DeviceIdType.MESH
BF = jnp.bfloat16
F32 = jnp.float32
I32 = jnp.int32
EXPERTS = 16
UNIT = 16

(DX, DG, GX, GG, SAB, SDH, AH, AD, RO, RX, BO, BX) = range(0, 24, 2)
(UX, LX, UG, LG) = range(24, 28)
PHASES = 28


def iotas(shape):
    return lax.broadcasted_iota(I32, shape, 0), lax.broadcasted_iota(I32, shape, 1)


def pick_table(rows, cols, mine, ne, routes, gates):
    expert, token = (rows >> 4) + mine - ne // 4, cols & 7
    expert = jnp.where(expert >= ne, expert - ne, jnp.where(expert < 0, expert + ne, expert))
    hot = jnp.zeros(rows.shape, F32)
    before = jnp.zeros(rows.shape, F32)
    gate = jnp.zeros(rows.shape, F32)
    for t in range(8):
        first, second = expert == routes[0, t], expert == routes[1, t]
        here = token == t
        named = jnp.where(first | second, 1.0, 0.0)
        hot = hot + jnp.where(here, named, 0.0)
        before = before + jnp.where(token > t, named, 0.0)
        weight = jnp.where(first, gates[0, t], 0.0) + jnp.where(second, gates[1, t], 0.0)
        gate = gate + jnp.where(here, weight, 0.0)
    slot = (rows & 1).astype(F32)
    keep = (((rows & 15) >> 1) == (cols >> 3)) & (before == slot)
    return jnp.where(keep, hot, 0.0), jnp.where(keep, gate, 0.0)


def stacked(value, chunks):
    parts = [value[:, j * 128 : (j + 1) * 128] for j in range(chunks)]
    parts = parts + [jnp.zeros_like(parts[0])] * (8 - chunks)
    return jnp.concatenate(parts, axis=0)


def kernel(
    sizes,
    tokens_in, cot_in, routes_in, gates_in, w_gate, w_up, w_down,
    mixed, d_tokens, d_gate, d_up, d_down,
    tokens, cot, routes, gates,
    slot_x, slot_g, got_x, got_g, via_x, via_g, all_x, all_g, w_in, w_out,
    part_ab, sum_ab, part_dh, sum_dh, hid, grads,
    out_s, out_r, dx_s, dx_r, back_os, back_or, back_xs, back_xr,
    grad_in, grad_out, spread,
    send, recv, loads,
):
    ne, ns, nl = sizes
    width = tokens.shape[1]
    chunks = width // 128
    hidden_n = w_gate.shape[1]
    quarter = ne // 4
    per = ne
    half = per * ns
    piece = half // nl
    half_units = ne // 2
    unit_rows = ne * UNIT
    node, loc = lax.axis_index("node"), lax.axis_index("local")
    expert, shard = node // ns, node % ns

    first = [
        pltpu.make_async_copy(routes_in, routes, loads.at[6]),
        pltpu.make_async_copy(gates_in, gates, loads.at[7]),
        pltpu.make_async_copy(tokens_in, tokens, loads.at[8]),
        pltpu.make_async_copy(cot_in, cot, loads.at[9]),
    ]
    fetch = [
        pltpu.make_async_copy(w_gate, w_in.at[:, pl.ds(0, hidden_n)], loads.at[0]),
        pltpu.make_async_copy(w_up, w_in.at[:, pl.ds(hidden_n, hidden_n)], loads.at[1]),
        pltpu.make_async_copy(w_down, w_out, loads.at[2]),
    ]
    for copy in first + fetch:
        copy.start()

    def at_expert(d):
        return lax.rem(expert + d % ne, ne) * ns + shard, loc

    near = [d for d in range(-quarter, quarter + 1) if d]
    by_shard = []
    for d in range(1, ns):
        other = lax.rem(shard + d, ns)
        by_shard.append((expert * ns + other, loc, other))
    by_local = []
    for d in range(1, nl):
        other = lax.rem(loc + d, nl)
        by_local.append((node, other, other))

    barrier = pltpu.get_barrier_semaphore()
    everyone = [(*at_expert(d), d) for d in near] + by_shard + by_local
    for to_node, to_loc, _ in everyone:
        pl.semaphore_signal(
            barrier, inc=1, device_id={"node": to_node, "local": to_loc}, device_id_type=MESH
        )

    def push(phase, peers, source, target):
        for to_node, to_loc, index in peers:
            pltpu.make_async_remote_copy(
                src_ref=source(index),
                dst_ref=target(index),
                send_sem=send.at[phase],
                recv_sem=recv.at[phase],
                device_id={"node": to_node, "local": to_loc},
                device_id_type=MESH,
            ).start()

    def arrived(phase, ref, count):
        if count > 0:
            part = ref.at[pl.ds(0, count)]
            pltpu.make_async_copy(part, part, recv.at[phase]).wait()

    def sent(phase, ref, count):
        if count > 0:
            part = ref.at[pl.ds(0, count)]
            pltpu.make_async_copy(part, part, send.at[phase]).wait()

    def span(h, index, n):
        return pl.ds(pl.multiple_of(h * half + index * n, n), n)

    def units(ref, index, count=1):
        return ref.at[pl.ds(index * UNIT, count * UNIT)]

    def spot(d):
        return (d + quarter) % ne

    def ship(phase, d, source, target):
        push(phase, [(*at_expert(d), 0)], lambda _: source, lambda _: target)

    for copy in first:
        copy.wait()
    member, weighted = pick_table(*iotas((unit_rows, 64)), expert, ne, routes, gates)
    pick = member.astype(BF)
    slot_gate = jnp.sum(weighted, axis=1, keepdims=True)
    tok = stacked(tokens[...].astype(F32), chunks).astype(BF)
    slot_x[...] = jnp.dot(pick, tok, preferred_element_type=F32).astype(BF)
    grad_rows = stacked(cot[...].astype(F32), chunks).astype(BF)
    slot_g[...] = (jnp.dot(pick, grad_rows, preferred_element_type=F32) * slot_gate).astype(BF)

    pl.semaphore_wait(barrier, len(everyone))
    n_up, n_low = quarter, quarter - 1
    up_at, low_at = spot(quarter + 1), spot(2 * quarter + 1)
    kinds = ((slot_x, got_x, via_x, DX, UX, LX), (slot_g, got_g, via_g, DG, UG, LG))
    for slots, got, via, straight, above, below in kinds:
        ship(above, quarter, units(slots, up_at, n_up), units(via, 0, n_up))
        if n_low:
            ship(below, -quarter, units(slots, low_at, n_low), units(via, n_up, n_low))
        ship(straight + 1, quarter, units(slots, spot(quarter)), units(got, spot(quarter)))
    for slots, got, via, straight, above, below in kinds:
        for d in sorted(near, key=lambda d: -abs(d)):
            if d != quarter:
                ship(straight, d, units(slots, spot(d)), units(got, spot(d)))
        own = spot(0) * UNIT
        got[own : own + UNIT, :] = slots[own : own + UNIT, :]

    a, b = iotas((chunks * per, half_units * UNIT))
    q = lax.rem(a, per)
    spread[...] = jnp.where(b == (q >> 1) * UNIT + 2 * (a // per) + (q & 1), 1.0, 0.0).astype(BF)

    for slots, got, via, straight, above, below in kinds:
        arrived(above, via, n_up * UNIT)
        for i in reversed(range(n_up)):
            ship(straight + 1, i + 1, units(via, i), units(got, up_at + i))
        arrived(below, via, n_low * UNIT)
        for i in range(n_low):
            ship(straight + 1, i - n_low, units(via, n_up + i), units(got, low_at + i))

    def gather(h, phase_in, phase_out, ref, target):
        arrived(phase_in + h, ref, (half_units - 1 + h) * UNIT)
        rows = ref[h * half_units * UNIT : (h + 1) * half_units * UNIT, :]
        flat = jnp.dot(spread[...], rows, preferred_element_type=F32).astype(BF)
        own_rows = span(h, shard, per)
        for j in range(chunks):
            target[own_rows, j * 128 : (j + 1) * 128] = flat[j * per : (j + 1) * per, :]
        push(phase_out + h, by_shard, lambda s: target.at[own_rows], lambda s: target.at[own_rows])

    def block(h):
        return slice(h * half, (h + 1) * half)

    def scatter(h, phase, part, where, peers, n, me):
        push(phase + h, peers, lambda i: part.at[span(h, i, n)], lambda i: where.at[span(h, me, n)])
        where[span(h, me, n), :] = part[span(h, me, n), :]

    def products(h):
        arrived(GX + h, all_x, (ns - 1) * per)
        part_ab[block(h), :] = jnp.dot(all_x[block(h), :], w_in[...], preferred_element_type=F32).astype(BF)
        scatter(h, SAB, part_ab, sum_ab, by_local, piece, loc)

    def hidden_grads(h):
        arrived(GG + h, all_g, (ns - 1) * per)
        part_dh[block(h), :] = lax.dot_general(
            all_g[block(h), :], w_out[...], (((1,), (1,)), ((), ())), preferred_element_type=F32
        ).astype(BF)
        scatter(h, SDH, part_dh, sum_dh, by_local, piece, loc)

    def total(ref, h, n, count):
        base = h * half
        value = ref[base : base + n, :].astype(F32)
        for i in range(1, count):
            value = value + ref[base + i * n : base + (i + 1) * n, :].astype(F32)
        return value

    def spread_local(h, phase, ref):
        mine = span(h, loc, piece)
        push(phase + h, by_local, lambda l: ref.at[mine], lambda l: ref.at[mine])

    kept = {}

    def activate(h):
        arrived(SAB + h, sum_ab, (nl - 1) * piece)
        ab = total(sum_ab, h, piece, nl)
        a_val, b_val = ab[:, :hidden_n], ab[:, hidden_n:]
        sig = jax.nn.sigmoid(a_val)
        kept[h] = (a_val, b_val, sig)
        hid[span(h, loc, piece), :] = (a_val * sig * b_val).astype(BF)
        spread_local(h, AH, hid)

    def differentiate(h):
        a_val, b_val, sig = kept[h]
        arrived(SDH + h, sum_dh, (nl - 1) * piece)
        dh = total(sum_dh, h, piece, nl)
        mine = span(h, loc, piece)
        grads[mine, 0:hidden_n] = (dh * b_val * sig * (1.0 + a_val * (1.0 - sig))).astype(BF)
        grads[mine, hidden_n : 2 * hidden_n] = (dh * a_val * sig).astype(BF)
        spread_local(h, AD, grads)

    def outputs(h):
        arrived(AH + h, hid, (nl - 1) * piece)
        out_s[block(h), :] = jnp.dot(hid[block(h), :], w_out[...], preferred_element_type=F32).astype(BF)
        scatter(h, RO, out_s, out_r, by_shard, per, shard)

    def input_grads(h):
        arrived(AD + h, grads, (nl - 1) * piece)
        dx_s[block(h), :] = lax.dot_general(
            grads[block(h), :], w_in[...], (((1,), (1,)), ((), ())), preferred_element_type=F32
        ).astype(BF)
        scatter(h, RX, dx_s, dx_r, by_shard, per, shard)

    def give_back(h, phase_in, phase_out, ref, source, target):
        arrived(phase_in + h, ref, (ns - 1) * per)
        value = total(ref, h, per, ns).astype(BF)
        tall = jnp.concatenate([value[:, j * 128 : (j + 1) * 128] for j in range(chunks)], axis=0)
        at = h * half_units * UNIT
        source[at : at + half_units * UNIT, :] = lax.dot_general(
            spread[...], tall, (((0,), (0,)), ((), ())), preferred_element_type=F32
        ).astype(BF)
        wanted = [d for d in range(-2 * quarter + 1, 2 * quarter + 1) if d and spot(d) // half_units == h]
        for d in sorted(wanted, key=lambda d: -abs(d)):
            ship(phase_out + h, -d, units(source, spot(d)), units(target, spot(d)))
        if h == 0:
            own = spot(0) * UNIT
            target[own : own + UNIT, :] = source[own : own + UNIT, :]

    gather(0, DX, GX, got_x, all_x)
    gather(0, DG, GG, got_g, all_g)
    for copy in fetch:
        copy.wait()
    gather(1, DX, GX, got_x, all_x)
    products(0)
    gather(1, DG, GG, got_g, all_g)
    hidden_grads(0)
    products(1)
    activate(0)
    hidden_grads(1)
    differentiate(0)
    activate(1)
    outputs(0)
    differentiate(1)
    input_grads(0)
    outputs(1)
    input_grads(1)
    give_back(0, RO, BO, out_r, back_os, back_or)
    give_back(0, RX, BX, dx_r, back_xs, back_xr)
    give_back(1, RO, BO, out_r, back_os, back_or)
    give_back(1, RX, BX, dx_r, back_xs, back_xr)

    over_rows = (((0,), (0,)), ((), ()))
    grad_out[...] = lax.dot_general(
        hid[...], all_g[...], over_rows, preferred_element_type=F32
    ).astype(BF)
    grad_in[...] = lax.dot_general(
        all_x[...], grads[...], over_rows, preferred_element_type=F32
    ).astype(BF)
    store = [
        pltpu.make_async_copy(grad_in.at[:, pl.ds(0, hidden_n)], d_gate, loads.at[3]),
        pltpu.make_async_copy(grad_in.at[:, pl.ds(hidden_n, hidden_n)], d_up, loads.at[4]),
        pltpu.make_async_copy(grad_out, d_down, loads.at[5]),
    ]
    for copy in store:
        copy.start()

    cols, tall_rows = iotas((64, unit_rows))
    member_t, weighted_t = pick_table(tall_rows, cols, expert, ne, routes, gates)
    high = weighted_t.astype(BF)
    low = (weighted_t - high.astype(F32)).astype(BF)

    for h in range(2):
        arrived(BO + h, back_or, (half_units - 1 + h) * UNIT)
    value = back_or[...]
    flat = jnp.dot(high, value, preferred_element_type=F32) + jnp.dot(
        low, value, preferred_element_type=F32
    )
    for j in range(chunks):
        mixed[:, j * 128 : (j + 1) * 128] = flat[j * 8 : (j + 1) * 8, :].astype(BF)
    for h in range(2):
        arrived(BX + h, back_xr, (half_units - 1 + h) * UNIT)
    flat = jnp.dot(member_t.astype(BF), back_xr[...], preferred_element_type=F32)
    for j in range(chunks):
        d_tokens[:, j * 128 : (j + 1) * 128] = flat[j * 8 : (j + 1) * 8, :].astype(BF)

    for above, below in ((UX, LX), (UG, LG)):
        sent(above, via_x, n_up * UNIT)
        sent(below, via_x, n_low * UNIT)
    for h in range(2):
        for phase in (DX, DG, BO, BX):
            sent(phase + h, slot_x, (half_units - 1 + h) * UNIT)
        for phase, ref in ((GX, all_x), (GG, all_g), (RO, out_s), (RX, dx_s)):
            sent(phase + h, ref, (ns - 1) * per)
        for phase, ref in ((SAB, part_ab), (SDH, part_dh), (AH, hid), (AD, grads)):
            sent(phase + h, ref, (nl - 1) * piece)
    for copy in store:
        copy.wait()


def place(*refs):
    count = len(refs) // 3
    source, target, held, done = refs[:count], refs[count : 2 * count], refs[2 * count : -1], refs[-1]
    reads = [pltpu.make_async_copy(source[i], held[i], done.at[i]) for i in range(count)]
    writes = [pltpu.make_async_copy(held[i], target[i], done.at[count + i]) for i in range(count)]
    for copy in reads:
        copy.start()
    for read, write in zip(reads, writes):
        read.wait()
        write.start()
    for copy in writes:
        copy.wait()


def local(sizes, tokens, cotangent, routes, gates, w_gate, w_up, w_down):
    ne, ns, nl = sizes
    toks, width = tokens.shape
    hidden_n = w_gate.shape[1]
    per = ne * 2
    rows_all = per * ns
    chunks = width // 128
    unit_rows = ne * UNIT
    vmem = pl.BlockSpec(memory_space=pltpu.VMEM)
    anywhere = pl.BlockSpec(memory_space=pl.ANY)
    unit = pltpu.VMEM((unit_rows, 128), BF)
    wide = pltpu.VMEM((rows_all, width), BF)
    scratch = (
        [pltpu.VMEM(tokens.shape, BF)] * 2
        + [pltpu.SMEM((2, toks), I32), pltpu.SMEM((2, toks), F32)]
        + [unit] * 4
        + [pltpu.VMEM((max(2, ne // 2 - 1) * UNIT, 128), BF)] * 2
        + [wide] * 2
        + [pltpu.VMEM((width, 2 * hidden_n), BF), pltpu.VMEM((hidden_n, width), BF)]
        + [pltpu.VMEM((rows_all, 2 * hidden_n), BF)] * 2
        + [pltpu.VMEM((rows_all, hidden_n), BF)] * 2
        + [pltpu.VMEM((rows_all, hidden_n), BF), pltpu.VMEM((rows_all, 2 * hidden_n), BF)]
        + [wide] * 4
        + [unit] * 4
        + [pltpu.VMEM((width, 2 * hidden_n), BF), pltpu.VMEM((hidden_n, width), BF)]
        + [pltpu.VMEM((chunks * ne, unit_rows // 2), BF)]
        + [pltpu.SemaphoreType.DMA((PHASES,)), pltpu.SemaphoreType.DMA((PHASES,)), pltpu.SemaphoreType.DMA((10,))]
    )
    shapes = (
            jax.ShapeDtypeStruct(tokens.shape, BF),
            jax.ShapeDtypeStruct(tokens.shape, BF),
            jax.ShapeDtypeStruct(w_gate.shape, BF),
            jax.ShapeDtypeStruct(w_up.shape, BF),
            jax.ShapeDtypeStruct(w_down.shape, BF),
    )
    results = pl.pallas_call(
        functools.partial(kernel, sizes),
        out_shape=shapes,
        in_specs=[anywhere] * 7,
        out_specs=(vmem, vmem, anywhere, anywhere, anywhere),
        scratch_shapes=scratch,
        compiler_params=pltpu.CompilerParams(
            collective_id=0, has_side_effects=True, vmem_limit_bytes=60 * 1024 * 1024
        ),
        cost_estimate=pl.CostEstimate(flops=1_100_000_000, bytes_accessed=3_000_000, transcendentals=8192),
    )(tokens, cotangent, routes.T, gates.T, w_gate, w_up, w_down)
    return pl.pallas_call(
        place,
        out_shape=shapes,
        in_specs=[anywhere] * 5,
        out_specs=(anywhere,) * 5,
        scratch_shapes=[pltpu.VMEM(r.shape, BF) for r in results] + [pltpu.SemaphoreType.DMA((10,))],
    )(*results)


def build(mesh, experts):
    shards = mesh.shape["node"] // experts
    sizes = (experts, shards, mesh.shape["local"])
    return jax.shard_map(
        functools.partial(local, sizes),
        mesh=mesh,
        in_specs=(
            P("node", "local"),
            P("node", "local"),
            P("node", None),
            P("node", None),
            P("local", "node"),
            P("local", "node"),
            P("node", "local"),
        ),
        out_specs=(
            P("node", "local"),
            P("node", "local"),
            P("local", "node"),
            P("local", "node"),
            P("node", "local"),
        ),
        check_vma=False,
    )


def solution(mesh):
    return build(mesh, EXPERTS)
```

```python
import functools

import jax
import jax.numpy as jnp
from jax import lax
from jax.experimental import pallas as pl
from jax.experimental.pallas import tpu as pltpu
from jax.sharding import PartitionSpec as P

MESH = pl.DeviceIdType.MESH
BF = jnp.bfloat16
F32 = jnp.float32
I32 = jnp.int32
EXPERTS = 16
UNIT = 16

(DX, DG, GX, GG, SAB, SDH, AH, AD, RO, RX, BO, BX) = range(0, 24, 2)
(UX, LX, UG, LG) = range(24, 28)
PHASES = 28


def iotas(shape):
    return lax.broadcasted_iota(I32, shape, 0), lax.broadcasted_iota(I32, shape, 1)


def pick_table(rows, cols, mine, ne, routes, gates):
    expert, token = (rows >> 4) + mine - ne // 4, cols & 7
    expert = jnp.where(expert >= ne, expert - ne, jnp.where(expert < 0, expert + ne, expert))
    hot = jnp.zeros(rows.shape, F32)
    before = jnp.zeros(rows.shape, F32)
    gate = jnp.zeros(rows.shape, F32)
    for t in range(8):
        first, second = expert == routes[0, t], expert == routes[1, t]
        here = token == t
        named = jnp.where(first | second, 1.0, 0.0)
        hot = hot + jnp.where(here, named, 0.0)
        before = before + jnp.where(token > t, named, 0.0)
        weight = jnp.where(first, gates[0, t], 0.0) + jnp.where(second, gates[1, t], 0.0)
        gate = gate + jnp.where(here, weight, 0.0)
    slot = (rows & 1).astype(F32)
    keep = (((rows & 15) >> 1) == (cols >> 3)) & (before == slot)
    return jnp.where(keep, hot, 0.0), jnp.where(keep, gate, 0.0)


def stacked(value, chunks):
    parts = [value[:, j * 128 : (j + 1) * 128] for j in range(chunks)]
    parts = parts + [jnp.zeros_like(parts[0])] * (8 - chunks)
    return jnp.concatenate(parts, axis=0)


def kernel(
    sizes,
    tokens_in, cot_in, routes_in, gates_in, w_gate, w_up, w_down,
    mixed, d_tokens, d_gate, d_up, d_down,
    tokens, cot, routes, gates,
    slot_x, slot_g, got_x, got_g, via_x, via_g, all_x, all_g, w_in, w_out,
    part_ab, sum_ab, part_dh, sum_dh, hid, grads,
    out_s, out_r, dx_s, dx_r, back_os, back_or, back_xs, back_xr,
    grad_in, grad_out, spread,
    send, recv, loads,
):
    ne, ns, nl = sizes
    width = tokens.shape[1]
    chunks = width // 128
    hidden_n = w_gate.shape[1]
    quarter = ne // 4
    per = ne
    half = per * ns
    piece = half // nl
    half_units = ne // 2
    unit_rows = ne * UNIT
    node, loc = lax.axis_index("node"), lax.axis_index("local")
    expert, shard = node // ns, node % ns

    first = [
        pltpu.make_async_copy(routes_in, routes, loads.at[6]),
        pltpu.make_async_copy(gates_in, gates, loads.at[7]),
        pltpu.make_async_copy(tokens_in, tokens, loads.at[8]),
        pltpu.make_async_copy(cot_in, cot, loads.at[9]),
    ]
    fetch = [
        pltpu.make_async_copy(w_gate, w_in.at[:, pl.ds(0, hidden_n)], loads.at[0]),
        pltpu.make_async_copy(w_up, w_in.at[:, pl.ds(hidden_n, hidden_n)], loads.at[1]),
        pltpu.make_async_copy(w_down, w_out, loads.at[2]),
    ]
    for copy in first + fetch:
        copy.start()

    def at_expert(d):
        return lax.rem(expert + d % ne, ne) * ns + shard, loc

    near = [d for d in range(-quarter, quarter + 1) if d]
    by_shard = []
    for d in sorted(range(1, ns), key=lambda d: -min(d % 4, 4 - d % 4)):
        other = lax.rem(shard + d, ns)
        by_shard.append((expert * ns + other, loc, other))
    by_local = []
    for d in sorted(range(1, nl), key=lambda d: -min(d, nl - d)):
        other = lax.rem(loc + d, nl)
        by_local.append((node, other, other))

    barrier = pltpu.get_barrier_semaphore()
    everyone = [(*at_expert(d), d) for d in near] + by_shard + by_local
    for to_node, to_loc, _ in everyone:
        pl.semaphore_signal(
            barrier, inc=1, device_id={"node": to_node, "local": to_loc}, device_id_type=MESH
        )

    def push(phase, peers, source, target):
        for to_node, to_loc, index in peers:
            pltpu.make_async_remote_copy(
                src_ref=source(index),
                dst_ref=target(index),
                send_sem=send.at[phase],
                recv_sem=recv.at[phase],
                device_id={"node": to_node, "local": to_loc},
                device_id_type=MESH,
            ).start()

    def arrived(phase, ref, count):
        if count > 0:
            part = ref.at[pl.ds(0, count)]
            pltpu.make_async_copy(part, part, recv.at[phase]).wait()

    def sent(phase, ref, count):
        if count > 0:
            part = ref.at[pl.ds(0, count)]
            pltpu.make_async_copy(part, part, send.at[phase]).wait()

    def span(h, index, n):
        return pl.ds(pl.multiple_of(h * half + index * n, n), n)

    def units(ref, index, count=1):
        return ref.at[pl.ds(index * UNIT, count * UNIT)]

    def spot(d):
        return (d + quarter) % ne

    def ship(phase, d, source, target):
        push(phase, [(*at_expert(d), 0)], lambda _: source, lambda _: target)

    for copy in first:
        copy.wait()
    member, weighted = pick_table(*iotas((unit_rows, 64)), expert, ne, routes, gates)
    pick = member.astype(BF)
    slot_gate = jnp.sum(weighted, axis=1, keepdims=True)
    tok = stacked(tokens[...].astype(F32), chunks).astype(BF)
    slot_x[...] = jnp.dot(pick, tok, preferred_element_type=F32).astype(BF)
    grad_rows = stacked(cot[...].astype(F32), chunks).astype(BF)
    slot_g[...] = (jnp.dot(pick, grad_rows, preferred_element_type=F32) * slot_gate).astype(BF)

    pl.semaphore_wait(barrier, len(everyone))
    n_up, n_low = quarter, quarter - 1
    up_at, low_at = spot(quarter + 1), spot(2 * quarter + 1)
    kinds = ((slot_x, got_x, via_x, DX, UX, LX), (slot_g, got_g, via_g, DG, UG, LG))
    for slots, got, via, straight, above, below in kinds:
        ship(above, quarter, units(slots, up_at, n_up), units(via, 0, n_up))
        if n_low:
            ship(below, -quarter, units(slots, low_at, n_low), units(via, n_up, n_low))
        ship(straight + 1, quarter, units(slots, spot(quarter)), units(got, spot(quarter)))
    for slots, got, via, straight, above, below in kinds:
        for d in sorted(near, key=lambda d: -abs(d)):
            if d != quarter:
                ship(straight, d, units(slots, spot(d)), units(got, spot(d)))
        own = spot(0) * UNIT
        got[own : own + UNIT, :] = slots[own : own + UNIT, :]

    a, b = iotas((chunks * per, half_units * UNIT))
    q = lax.rem(a, per)
    spread[...] = jnp.where(b == (q >> 1) * UNIT + 2 * (a // per) + (q & 1), 1.0, 0.0).astype(BF)

    for slots, got, via, straight, above, below in kinds:
        arrived(above, via, n_up * UNIT)
        for i in reversed(range(n_up)):
            ship(straight + 1, i + 1, units(via, i), units(got, up_at + i))
        arrived(below, via, n_low * UNIT)
        for i in range(n_low):
            ship(straight + 1, i - n_low, units(via, n_up + i), units(got, low_at + i))

    def gather(h, phase_in, phase_out, ref, target):
        arrived(phase_in + h, ref, (half_units - 1 + h) * UNIT)
        rows = ref[h * half_units * UNIT : (h + 1) * half_units * UNIT, :]
        flat = jnp.dot(spread[...], rows, preferred_element_type=F32).astype(BF)
        own_rows = span(h, shard, per)
        for j in range(chunks):
            target[own_rows, j * 128 : (j + 1) * 128] = flat[j * per : (j + 1) * per, :]
        push(phase_out + h, by_shard, lambda s: target.at[own_rows], lambda s: target.at[own_rows])

    def block(h):
        return slice(h * half, (h + 1) * half)

    def scatter(h, phase, part, where, peers, n, me):
        push(phase + h, peers, lambda i: part.at[span(h, i, n)], lambda i: where.at[span(h, me, n)])
        where[span(h, me, n), :] = part[span(h, me, n), :]

    def products(h):
        arrived(GX + h, all_x, (ns - 1) * per)
        part_ab[block(h), :] = jnp.dot(all_x[block(h), :], w_in[...], preferred_element_type=F32).astype(BF)
        scatter(h, SAB, part_ab, sum_ab, by_local, piece, loc)

    def hidden_grads(h):
        arrived(GG + h, all_g, (ns - 1) * per)
        part_dh[block(h), :] = lax.dot_general(
            all_g[block(h), :], w_out[...], (((1,), (1,)), ((), ())), preferred_element_type=F32
        ).astype(BF)
        scatter(h, SDH, part_dh, sum_dh, by_local, piece, loc)

    def total(ref, h, n, count):
        base = h * half
        value = ref[base : base + n, :].astype(F32)
        for i in range(1, count):
            value = value + ref[base + i * n : base + (i + 1) * n, :].astype(F32)
        return value

    def spread_local(h, phase, ref):
        mine = span(h, loc, piece)
        push(phase + h, by_local, lambda l: ref.at[mine], lambda l: ref.at[mine])

    kept = {}

    def activate(h):
        arrived(SAB + h, sum_ab, (nl - 1) * piece)
        ab = total(sum_ab, h, piece, nl)
        a_val, b_val = ab[:, :hidden_n], ab[:, hidden_n:]
        sig = jax.nn.sigmoid(a_val)
        kept[h] = (a_val, b_val, sig)
        hid[span(h, loc, piece), :] = (a_val * sig * b_val).astype(BF)
        spread_local(h, AH, hid)

    def differentiate(h):
        a_val, b_val, sig = kept[h]
        arrived(SDH + h, sum_dh, (nl - 1) * piece)
        dh = total(sum_dh, h, piece, nl)
        mine = span(h, loc, piece)
        grads[mine, 0:hidden_n] = (dh * b_val * sig * (1.0 + a_val * (1.0 - sig))).astype(BF)
        grads[mine, hidden_n : 2 * hidden_n] = (dh * a_val * sig).astype(BF)
        spread_local(h, AD, grads)

    def outputs(h):
        arrived(AH + h, hid, (nl - 1) * piece)
        out_s[block(h), :] = jnp.dot(hid[block(h), :], w_out[...], preferred_element_type=F32).astype(BF)
        scatter(h, RO, out_s, out_r, by_shard, per, shard)

    def input_grads(h):
        arrived(AD + h, grads, (nl - 1) * piece)
        dx_s[block(h), :] = lax.dot_general(
            grads[block(h), :], w_in[...], (((1,), (1,)), ((), ())), preferred_element_type=F32
        ).astype(BF)
        scatter(h, RX, dx_s, dx_r, by_shard, per, shard)

    def give_back(h, phase_in, phase_out, ref, source, target):
        arrived(phase_in + h, ref, (ns - 1) * per)
        value = total(ref, h, per, ns).astype(BF)
        tall = jnp.concatenate([value[:, j * 128 : (j + 1) * 128] for j in range(chunks)], axis=0)
        at = h * half_units * UNIT
        source[at : at + half_units * UNIT, :] = lax.dot_general(
            spread[...], tall, (((0,), (0,)), ((), ())), preferred_element_type=F32
        ).astype(BF)
        wanted = [d for d in range(-2 * quarter + 1, 2 * quarter + 1) if d and spot(d) // half_units == h]
        for d in sorted(wanted, key=lambda d: -abs(d)):
            ship(phase_out + h, -d, units(source, spot(d)), units(target, spot(d)))
        if h == 0:
            own = spot(0) * UNIT
            target[own : own + UNIT, :] = source[own : own + UNIT, :]

    gather(0, DX, GX, got_x, all_x)
    gather(0, DG, GG, got_g, all_g)
    for copy in fetch:
        copy.wait()
    gather(1, DX, GX, got_x, all_x)
    products(0)
    gather(1, DG, GG, got_g, all_g)
    hidden_grads(0)
    activate(0)
    products(1)
    hidden_grads(1)
    activate(1)
    differentiate(0)
    outputs(0)
    outputs(1)
    differentiate(1)
    input_grads(0)
    input_grads(1)
    give_back(0, RO, BO, out_r, back_os, back_or)
    give_back(1, RO, BO, out_r, back_os, back_or)
    give_back(0, RX, BX, dx_r, back_xs, back_xr)
    give_back(1, RX, BX, dx_r, back_xs, back_xr)

    over_rows = (((0,), (0,)), ((), ()))
    grad_out[...] = lax.dot_general(
        hid[...], all_g[...], over_rows, preferred_element_type=F32
    ).astype(BF)
    grad_in[...] = lax.dot_general(
        all_x[...], grads[...], over_rows, preferred_element_type=F32
    ).astype(BF)
    store = [
        pltpu.make_async_copy(grad_in.at[:, pl.ds(0, hidden_n)], d_gate, loads.at[3]),
        pltpu.make_async_copy(grad_in.at[:, pl.ds(hidden_n, hidden_n)], d_up, loads.at[4]),
        pltpu.make_async_copy(grad_out, d_down, loads.at[5]),
    ]
    for copy in store:
        copy.start()

    cols, tall_rows = iotas((64, unit_rows))
    member_t, weighted_t = pick_table(tall_rows, cols, expert, ne, routes, gates)
    high = weighted_t.astype(BF)
    low = (weighted_t - high.astype(F32)).astype(BF)

    for h in range(2):
        arrived(BO + h, back_or, (half_units - 1 + h) * UNIT)
    value = back_or[...]
    flat = jnp.dot(high, value, preferred_element_type=F32) + jnp.dot(
        low, value, preferred_element_type=F32
    )
    for j in range(chunks):
        mixed[:, j * 128 : (j + 1) * 128] = flat[j * 8 : (j + 1) * 8, :].astype(BF)
    for h in range(2):
        arrived(BX + h, back_xr, (half_units - 1 + h) * UNIT)
    flat = jnp.dot(member_t.astype(BF), back_xr[...], preferred_element_type=F32)
    for j in range(chunks):
        d_tokens[:, j * 128 : (j + 1) * 128] = flat[j * 8 : (j + 1) * 8, :].astype(BF)

    for above, below in ((UX, LX), (UG, LG)):
        sent(above, via_x, n_up * UNIT)
        sent(below, via_x, n_low * UNIT)
    for h in range(2):
        for phase in (DX, DG, BO, BX):
            sent(phase + h, slot_x, (half_units - 1 + h) * UNIT)
        for phase, ref in ((GX, all_x), (GG, all_g), (RO, out_s), (RX, dx_s)):
            sent(phase + h, ref, (ns - 1) * per)
        for phase, ref in ((SAB, part_ab), (SDH, part_dh), (AH, hid), (AD, grads)):
            sent(phase + h, ref, (nl - 1) * piece)
    for copy in store:
        copy.wait()


def place(*refs):
    count = len(refs) // 3
    source, target, held, done = refs[:count], refs[count : 2 * count], refs[2 * count : -1], refs[-1]
    reads = [pltpu.make_async_copy(source[i], held[i], done.at[i]) for i in range(count)]
    writes = [pltpu.make_async_copy(held[i], target[i], done.at[count + i]) for i in range(count)]
    for copy in reads:
        copy.start()
    for read, write in zip(reads, writes):
        read.wait()
        write.start()
    for copy in writes:
        copy.wait()


def local(sizes, tokens, cotangent, routes, gates, w_gate, w_up, w_down):
    ne, ns, nl = sizes
    toks, width = tokens.shape
    hidden_n = w_gate.shape[1]
    per = ne * 2
    rows_all = per * ns
    chunks = width // 128
    unit_rows = ne * UNIT
    vmem = pl.BlockSpec(memory_space=pltpu.VMEM)
    anywhere = pl.BlockSpec(memory_space=pl.ANY)
    unit = pltpu.VMEM((unit_rows, 128), BF)
    wide = pltpu.VMEM((rows_all, width), BF)
    scratch = (
        [pltpu.VMEM(tokens.shape, BF)] * 2
        + [pltpu.SMEM((2, toks), I32), pltpu.SMEM((2, toks), F32)]
        + [unit] * 4
        + [pltpu.VMEM((max(2, ne // 2 - 1) * UNIT, 128), BF)] * 2
        + [wide] * 2
        + [pltpu.VMEM((width, 2 * hidden_n), BF), pltpu.VMEM((hidden_n, width), BF)]
        + [pltpu.VMEM((rows_all, 2 * hidden_n), BF)] * 2
        + [pltpu.VMEM((rows_all, hidden_n), BF)] * 2
        + [pltpu.VMEM((rows_all, hidden_n), BF), pltpu.VMEM((rows_all, 2 * hidden_n), BF)]
        + [wide] * 4
        + [unit] * 4
        + [pltpu.VMEM((width, 2 * hidden_n), BF), pltpu.VMEM((hidden_n, width), BF)]
        + [pltpu.VMEM((chunks * ne, unit_rows // 2), BF)]
        + [pltpu.SemaphoreType.DMA((PHASES,)), pltpu.SemaphoreType.DMA((PHASES,)), pltpu.SemaphoreType.DMA((10,))]
    )
    shapes = (
            jax.ShapeDtypeStruct(tokens.shape, BF),
            jax.ShapeDtypeStruct(tokens.shape, BF),
            jax.ShapeDtypeStruct(w_gate.shape, BF),
            jax.ShapeDtypeStruct(w_up.shape, BF),
            jax.ShapeDtypeStruct(w_down.shape, BF),
    )
    results = pl.pallas_call(
        functools.partial(kernel, sizes),
        out_shape=shapes,
        in_specs=[anywhere] * 7,
        out_specs=(vmem, vmem, anywhere, anywhere, anywhere),
        scratch_shapes=scratch,
        compiler_params=pltpu.CompilerParams(
            collective_id=0, has_side_effects=True, vmem_limit_bytes=60 * 1024 * 1024
        ),
        cost_estimate=pl.CostEstimate(flops=1_100_000_000, bytes_accessed=3_000_000, transcendentals=8192),
    )(tokens, cotangent, routes.T, gates.T, w_gate, w_up, w_down)
    return pl.pallas_call(
        place,
        out_shape=shapes,
        in_specs=[anywhere] * 5,
        out_specs=(anywhere,) * 5,
        scratch_shapes=[pltpu.VMEM(r.shape, BF) for r in results] + [pltpu.SemaphoreType.DMA((10,))],
    )(*results)


def build(mesh, experts):
    shards = mesh.shape["node"] // experts
    sizes = (experts, shards, mesh.shape["local"])
    return jax.shard_map(
        functools.partial(local, sizes),
        mesh=mesh,
        in_specs=(
            P("node", "local"),
            P("node", "local"),
            P("node", None),
            P("node", None),
            P("local", "node"),
            P("local", "node"),
            P("node", "local"),
        ),
        out_specs=(
            P("node", "local"),
            P("node", "local"),
            P("local", "node"),
            P("local", "node"),
            P("node", "local"),
        ),
        check_vma=False,
    )


def solution(mesh):
    return build(mesh, EXPERTS)
```
